32 devices in a mesh: section: 8 (over z, x), tensor: 4 (over y, core).
Axes of the slice: x: 2, y: 2, z: 4, core: 2. Of those that a mesh axis runs over, the one named last changes fastest.
Arguments:
- tree_queries: bfloat16 [8, 32, 4, 16384], P('section', 'tensor'), may hold values from -8 to 8
- tree_kv: bfloat16 [8, 32, 4, 2, 1024], P('section', 'tensor'), may hold values from -8 to 8
- cache_kv: bfloat16 [8, 32, 96, 2, 1024], P('section', 'tensor'), may hold values from -8 to 8
- residual: bfloat16 [8, 32, 4, 16384], P('section', 'tensor'), may hold values from -24 to 24
- cache_lengths: int32 [32], P('tensor'), may hold values from 12 to 96
- tree_parents: int32 [32, 4], P('tensor'), may hold values from -1 to 2, as said below
- accepted: int32 [32], P('tensor'), may hold values from 0 to 4
- merging_weight: bfloat16 [3, 16384, 16384], P(None, 'section', 'tensor')
- merging_gain: bfloat16 [16384], P('tensor'), may hold values from 0.25 to 1.75
Outputs:
- verified: bfloat16 [8, 32, 4, 16384], P('section', 'tensor')
- draft_input: bfloat16 [32, 4, 16384], P('section', None, 'tensor')
The draws below stay inside these ranges and needn't reach their ends.
Inputs may be any that keep to these rules, and one draw needn't show every extreme that they name: tree_parents[r, 0] = -1, and for t >= 1 tree_parents[r, t] lies in 0 .. t - 1.
All inputs are finite; a program needn't handle non-finite values.
Results may differ from the reference program's by a relative error of at most 0.005.
Values may be sent and summed in bfloat16 or wider, within the bound.
A program may use at most 128 MiB of HBM per device.

```python
import math
import jax
import jax.numpy as jnp
from jax import lax

D = 16384
HEADS = 128
KV_HEADS = 8
HEAD_DIM = 128
TREE = 4
CACHE = 96
GROUP_ROWS = 32
N_SECTION = 8


def query_base(key):
    shape = (N_SECTION, GROUP_ROWS, TREE, HEADS, HEAD_DIM)
    base_key = jax.random.fold_in(key, 7)
    values = jnp.clip(jax.random.normal(base_key, shape, jnp.float32), -6.0, 6.0)
    return values


def draw_tree_queries(key, part):
    base = query_base(key)
    return base.reshape(N_SECTION, GROUP_ROWS, TREE, D).astype(jnp.bfloat16)


def draw_tree_kv(key, part):
    group_size = HEADS // KV_HEADS
    base = query_base(key).reshape(N_SECTION, GROUP_ROWS, TREE, KV_HEADS, group_size, HEAD_DIM)
    boost = jnp.sum(base, axis=4) * (3.0 / group_size)
    noise_key, value_key = jax.random.split(jax.random.fold_in(key, 13))
    shape = (N_SECTION, GROUP_ROWS, TREE, KV_HEADS, HEAD_DIM)
    keys_part = jnp.clip(jax.random.normal(noise_key, shape, jnp.float32) + boost, -8.0, 8.0)
    values_part = jnp.clip(3.0 * jax.random.normal(value_key, shape, jnp.float32), -8.0, 8.0)
    stacked = jnp.stack([keys_part.reshape(N_SECTION, GROUP_ROWS, TREE, KV_HEADS * HEAD_DIM), values_part.reshape(N_SECTION, GROUP_ROWS, TREE, KV_HEADS * HEAD_DIM)], axis=3)
    return stacked.astype(jnp.bfloat16)


def draw_cache_kv(key, part):
    noise_key, value_key = jax.random.split(jax.random.fold_in(key, 17))
    shape = (N_SECTION, GROUP_ROWS, CACHE, KV_HEADS, HEAD_DIM)
    values_part = jnp.clip(3.0 * jax.random.normal(value_key, shape, jnp.float32), -8.0, 8.0)
    keys_part = jnp.clip(jax.random.normal(noise_key, shape, jnp.float32), -6.0, 6.0)
    stacked = jnp.stack([keys_part.reshape(N_SECTION, GROUP_ROWS, CACHE, KV_HEADS * HEAD_DIM), values_part.reshape(N_SECTION, GROUP_ROWS, CACHE, KV_HEADS * HEAD_DIM)], axis=3)
    return stacked.astype(jnp.bfloat16)


def draw_residual(key, part):
    noise_key, scale_key = jax.random.split(jax.random.fold_in(key, 19))
    shape = (N_SECTION, GROUP_ROWS, TREE, D)
    noise = jnp.clip(jax.random.normal(noise_key, shape, jnp.float32), -4.0, 4.0)
    row_scale = jnp.exp(jax.random.uniform(scale_key, (N_SECTION, GROUP_ROWS, TREE, 1), jnp.float32, math.log(0.3), math.log(3.0)))
    return (noise * row_scale).astype(jnp.bfloat16)


def draw_merging_weight(key, part):
    noise_key, jitter_key = jax.random.split(jax.random.fold_in(key, 23), 2)
    column = jnp.arange(D, dtype=jnp.float32) / D
    jitter = jnp.exp(jax.random.uniform(jitter_key, (D,), jnp.float32, -0.35, 0.35))
    base = jnp.clip(jax.random.normal(noise_key, (3 * D, D), jnp.float32), -4.0, 4.0)
    column_scale = 10.0 ** column * jitter
    weight = base * column_scale[None, :] * (1.0 / math.sqrt(3 * D))
    return weight.reshape(3, D, D).astype(jnp.bfloat16)


def draw_tree_parents(key, part):
    position = jnp.arange(TREE, dtype=jnp.int32)[None, :]
    upper = jnp.maximum(position, 1)
    drawn = jax.random.randint(jax.random.fold_in(key, 29), (GROUP_ROWS, TREE), 0, upper)
    return jnp.where(position == 0, -1, drawn).astype(jnp.int32)


def draw_cache_lengths(key, part):
    long_key, short_key, pick_key, forced_key = jax.random.split(jax.random.fold_in(key, 31), 4)
    short_rows = jax.random.randint(short_key, (GROUP_ROWS,), CACHE // 8, CACHE // 2 + 1)
    long_rows = jax.random.randint(long_key, (GROUP_ROWS,), CACHE // 2, CACHE + 1)
    picked = jax.random.randint(pick_key, (GROUP_ROWS,), 0, 8) == 0
    lengths = jnp.where(picked, long_rows, short_rows)
    forced_row = jax.random.randint(forced_key, (), 0, GROUP_ROWS)
    lengths = jnp.where(jnp.arange(GROUP_ROWS, dtype=jnp.int32) == forced_row, CACHE, lengths)
    return lengths.astype(jnp.int32)


def plant(values, rng, low, high):
    spot = [jax.random.randint(jax.random.fold_in(rng, axis), (), 0, length) for axis, length in enumerate(values.shape)]
    main_axis = values.shape.index(max(values.shape))
    beside = spot[:main_axis] + [(spot[main_axis] + 1) % values.shape[main_axis]] + spot[main_axis + 1:]
    return values.at[tuple(spot)].set(low).at[tuple(beside)].set(high)


def setup_inputs(seed: int = 0) -> dict:
    keys = jax.random.split(jax.random.key(seed), 10)
    return {
        "tree_queries": draw_tree_queries(jax.random.fold_in(keys[9], 71), 0),
        "tree_kv": draw_tree_kv(jax.random.fold_in(keys[9], 71), 0),
        "cache_kv": draw_cache_kv(jax.random.fold_in(keys[9], 71), 0),
        "residual": draw_residual(jax.random.fold_in(keys[9], 71), 0),
        "cache_lengths": draw_cache_lengths(jax.random.fold_in(keys[9], 71), 0),
        "tree_parents": draw_tree_parents(jax.random.fold_in(keys[9], 71), 0),
        "accepted": plant(jax.random.randint(keys[6], (GROUP_ROWS,), 0, TREE + 1), jax.random.fold_in(keys[6], 1), 0, TREE).astype(jnp.int32),
        "merging_weight": draw_merging_weight(jax.random.fold_in(keys[9], 71), 0),
        "merging_gain": jnp.clip(1.0 + 0.15 * jax.random.normal(keys[8], (D,), jnp.float32), 0.25, 1.75).astype(jnp.bfloat16),
    }


def ancestors(parents):
    row_count, tokens = parents.shape
    identity = jnp.eye(tokens, dtype=jnp.float32)
    token_ids = jnp.arange(tokens, dtype=jnp.int32)
    lineage_rows = [jnp.broadcast_to(identity[0], (row_count, tokens))]
    for token_index in range(1, tokens):
        parent_hot = (parents[:, token_index][:, None] == token_ids[None, :]).astype(jnp.float32)
        earlier = jnp.stack(lineage_rows, axis=1)
        inherited = jnp.einsum('ru,ruv->rv', parent_hot[:, :token_index], earlier)
        lineage_rows.append(jnp.maximum(inherited, identity[token_index][None, :]))
    return jnp.stack(lineage_rows, axis=1)

def group_attention(queries, tree_kv, cache_kv, residual, lengths, lineage):
    row_count = queries.shape[0]
    group_size = HEADS // KV_HEADS
    factor = HEAD_DIM ** (-0.5)
    highest = lax.Precision.HIGHEST
    grouped = queries.reshape(row_count, TREE, KV_HEADS, group_size, HEAD_DIM).astype(jnp.float32)
    own_keys = tree_kv[:, :, 0].reshape(row_count, TREE, KV_HEADS, HEAD_DIM).astype(jnp.float32)
    own_values = tree_kv[:, :, 1].reshape(row_count, TREE, KV_HEADS, HEAD_DIM).astype(jnp.float32)
    cache_keys = cache_kv[:, :, 0].reshape(row_count, CACHE, KV_HEADS, HEAD_DIM).astype(jnp.float32)
    cache_values = cache_kv[:, :, 1].reshape(row_count, CACHE, KV_HEADS, HEAD_DIM).astype(jnp.float32)
    tree_scores = jnp.einsum('rtkgd,rukd->rtkgu', grouped, own_keys, precision=highest) * factor
    tree_scores = jnp.where(lineage[:, :, None, None, :] > 0.5, tree_scores, -jnp.inf)
    cache_scores = jnp.einsum('rtkgd,rskd->rtkgs', grouped, cache_keys, precision=highest) * factor
    in_cache = jnp.arange(CACHE, dtype=jnp.int32)[None, :] < lengths[:, None]
    cache_scores = jnp.where(in_cache[:, None, None, None, :], cache_scores, -jnp.inf)
    scores = jnp.concatenate([cache_scores, tree_scores], axis=-1)
    weights = jax.nn.softmax(scores, axis=-1)
    values = jnp.concatenate([cache_values, own_values], axis=1)
    attention = jnp.einsum('rtkgs,rskd->rtkgd', weights, values, precision=highest)
    return (residual.astype(jnp.float32) + attention.reshape(row_count, TREE, D)).astype(jnp.bfloat16)

def reference(tree_queries, tree_kv, cache_kv, residual, cache_lengths, tree_parents, accepted, merging_weight, merging_gain):
    lineage = ancestors(tree_parents)

    def one_group(inputs):
        return group_attention(inputs[0], inputs[1], inputs[2], inputs[3], cache_lengths, lineage)
    verified = lax.map(one_group, (tree_queries, tree_kv, cache_kv, residual))
    accepted_mask = (jnp.arange(TREE, dtype=jnp.int32)[None, :] < accepted[:, None])[:, :, None]
    captured = [jnp.where(accepted_mask, verified[group_id], jnp.zeros((), jnp.bfloat16)) for group_id in (0, N_SECTION // 2, N_SECTION - 1)]
    joined = jnp.concatenate(captured, axis=-1).reshape(GROUP_ROWS * TREE, 3 * D)
    merged = jnp.dot(joined, merging_weight.reshape(3 * D, D), preferred_element_type=jnp.float32)
    inverse_rms = lax.rsqrt(lax.optimization_barrier(jnp.mean(merged * merged, axis=-1, keepdims=True)) + 1e-05)
    draft_input = (merged * inverse_rms * merging_gain.astype(jnp.float32)[None, :]).astype(jnp.bfloat16)
    return (verified, draft_input.reshape(GROUP_ROWS, TREE, D))
```

```python
import functools

import jax
import jax.numpy as jnp
from jax import lax
from jax.experimental import pallas as pl
from jax.experimental.pallas import tpu as pltpu
from jax.sharding import PartitionSpec as P

KV_HEADS = 8
HEAD_DIM = 128
MESH = pl.DeviceIdType.MESH
F32 = jnp.float32
BF16 = jnp.bfloat16


def attention_kernel(
    lengths_ref,
    parents_ref,
    accepted_ref,
    query_ref,
    cache_ref,
    tree_ref,
    residual_ref,
    verified_ref,
    captured_ref,
    kv_scr,
    head_scr,
    token_scr,
    captured_scr,
):
    row = pl.program_id(0)
    tokens = query_ref.shape[1]
    cached = cache_ref.shape[1]
    own = tree_ref.shape[1]
    span = kv_scr.shape[0]
    heads = query_ref.shape[2] // HEAD_DIM
    group = heads // KV_HEADS
    lines = group * tokens

    kv_scr[0:cached] = cache_ref[0]
    kv_scr[cached:span] = jnp.zeros((span - cached, kv_scr.shape[1]), BF16)
    kv_scr[cached : cached + own] = tree_ref[0]

    for head in range(heads):
        head_scr[head * tokens : (head + 1) * tokens, :] = query_ref[
            0, :, head * HEAD_DIM : (head + 1) * HEAD_DIM
        ].astype(F32)

    bits = [jnp.int32(1)]
    for token in range(1, tokens):
        parent = parents_ref[row, token]
        inherited = jnp.int32(0)
        for earlier in range(token):
            inherited = jnp.where(parent == earlier, bits[earlier], inherited)
        bits.append(inherited | (1 << token))
    token_id = lax.broadcasted_iota(jnp.int32, (lines, span), 0) % tokens
    column = lax.broadcasted_iota(jnp.int32, (lines, span), 1)
    line_bits = jnp.full((lines, span), bits[0], jnp.int32)
    for token in range(1, tokens):
        line_bits = jnp.where(token_id == token, bits[token], line_bits)
    own_index = jnp.clip((column - cached) // 2, 0, 31)
    in_tree = (
        (column >= cached)
        & (column < cached + own)
        & ((lax.shift_right_logical(line_bits, own_index) & 1) == 1)
    )
    in_cache = column < jnp.minimum(2 * lengths_ref[row], cached)
    allowed = (in_cache | in_tree) & (column % 2 == 0)

    factor = HEAD_DIM ** (-0.5)
    scores = []
    for kv in range(KV_HEADS):
        queries = head_scr[kv * lines : (kv + 1) * lines, :].astype(BF16)
        keys = kv_scr[:, kv * HEAD_DIM : (kv + 1) * HEAD_DIM]
        scores.append(
            lax.dot_general(
                queries, keys, (((1,), (1,)), ((), ())), preferred_element_type=F32
            )
        )
    for kv in range(KV_HEADS):
        score = jnp.where(allowed, scores[kv] * factor, -jnp.inf)
        weights = jnp.exp(score - jnp.max(score, axis=1, keepdims=True))
        total = jnp.sum(weights, axis=1, keepdims=True)
        shifted = pltpu.roll(weights, 1, 1).astype(BF16)
        weighted = jnp.dot(
            shifted,
            kv_scr[:, kv * HEAD_DIM : (kv + 1) * HEAD_DIM],
            preferred_element_type=F32,
        )
        head_scr[kv * lines : (kv + 1) * lines, :] = weighted / total

    keep = lax.broadcasted_iota(jnp.int32, (tokens, HEAD_DIM), 0) < accepted_ref[row]
    for head in range(heads):
        features = slice(head * HEAD_DIM, (head + 1) * HEAD_DIM)
        summed = (
            residual_ref[0, :, features].astype(F32)
            + head_scr[head * tokens : (head + 1) * tokens, :]
        )
        verified_ref[0, :, features] = summed.astype(BF16)
        token_scr[:, features] = jnp.where(keep, summed, 0.0)

    shared = captured_scr.shape[1] // tokens
    for place in range(shared):

        @pl.when(row % shared == place)
        def _(place=place):
            captured_scr[row // shared, place * tokens : (place + 1) * tokens, :] = token_scr[...]

    @pl.when(row == pl.num_programs(0) - 1)
    def _():
        captured_ref[...] = captured_scr[...].reshape(captured_ref.shape).astype(BF16)


def attend(queries, tree_kv, cache_kv, residual, lengths, parents, accepted):
    rows, tokens, width = queries.shape
    cached = 2 * cache_kv.shape[1]
    own = 2 * tokens
    span = -(-(cached + own) // 128) * 128
    kv_width = cache_kv.shape[3]
    row_block = lambda *shape: pl.BlockSpec((1,) + shape, lambda r: (r, 0, 0))
    scalars = pl.BlockSpec(memory_space=pltpu.SMEM)
    return pl.pallas_call(
        attention_kernel,
        grid=(rows,),
        out_shape=(
            jax.ShapeDtypeStruct((rows, tokens, width), BF16),
            jax.ShapeDtypeStruct((rows * tokens, width), BF16),
        ),
        in_specs=[
            scalars,
            scalars,
            scalars,
            row_block(tokens, width),
            row_block(cached, kv_width),
            row_block(own, kv_width),
            row_block(tokens, width),
        ],
        out_specs=(
            row_block(tokens, width),
            pl.BlockSpec((rows * tokens, width), lambda r: (0, 0)),
        ),
        scratch_shapes=[
            pltpu.VMEM((span, kv_width), BF16),
            pltpu.VMEM((width // HEAD_DIM * tokens, HEAD_DIM), F32),
            pltpu.VMEM((tokens, width), F32),
            pltpu.VMEM((rows * tokens // 8, 8, width), F32),
        ],
        compiler_params=pltpu.CompilerParams(vmem_limit_bytes=32 * 2**20),
        name="tree_attention",
    )(
        lengths,
        parents,
        accepted,
        queries,
        cache_kv.reshape(rows, cached, kv_width),
        tree_kv.reshape(rows, own, kv_width),
        residual,
    )


LAG = 2


def merge_kernel(
    sections,
    tensors,
    captured_ref,
    weight_ref,
    gain_ref,
    out_ref,
    weight_v,
    captured_v,
    sums,
    own,
    pair_out,
    pair_in,
    line_out,
    line_in,
    final,
    squares,
    weight_sem,
    local_sem,
    root_send,
    root_recv,
    row_send,
    row_recv,
    core_send,
    core_recv,
    pair_send,
    pair_recv,
    line_send,
    line_recv,
    square_send,
    square_recv,
):
    section = lax.axis_index("section")
    tensor = lax.axis_index("tensor")
    chunks, groups, block, width = weight_v.shape
    rows = captured_ref.shape[0]
    line = sections // 2
    out_rows = out_ref.shape[0]
    place, parity = section // 2, section % 2
    partner = section + 1 - 2 * parity
    other_core = tensor + 1 - 2 * (tensor % 2)
    roots = (0, sections // 2, sections - 1)

    def remote(src, dst, send, recv, to_section, to_tensor):
        return pltpu.make_async_remote_copy(
            src_ref=src,
            dst_ref=dst,
            send_sem=send,
            recv_sem=recv,
            device_id=(to_section, to_tensor),
            device_id_type=MESH,
        )

    def weight_copy(chunk):
        columns = pl.ds(pl.multiple_of(chunk * width, width), width)
        return pltpu.make_async_copy(
            weight_ref.at[:, :, columns], weight_v.at[chunk], weight_sem.at[chunk]
        )

    for chunk in range(chunks):
        weight_copy(chunk).start()

    barrier = pltpu.get_barrier_semaphore()
    for step in range(1, sections):
        pl.semaphore_signal(
            barrier, inc=1, device_id=((section + step) % sections, tensor), device_id_type=MESH
        )
    for step in range(1, tensors):
        pl.semaphore_signal(
            barrier, inc=1, device_id=(section, (tensor + step) % tensors), device_id_type=MESH
        )
    pl.semaphore_wait(barrier, sections + tensors - 2)

    def piece(group, owner):
        return captured_v.at[group, pl.ds(pl.multiple_of(owner * rows, rows), rows), :]

    def features(to_section):
        return captured_ref.at[:, pl.ds(pl.multiple_of(to_section * block, block), block)]

    def root_copy(group, step):
        to_section = (section + step) % sections
        return remote(
            features(to_section),
            piece(group, tensor),
            root_send.at[step - 1],
            root_recv.at[group],
            to_section,
            tensor,
        )

    def root_local(group):
        return pltpu.make_async_copy(features(section), piece(group, tensor), local_sem)

    for group, root in enumerate(roots):

        @pl.when(section == root)
        def _(group=group):
            for step in range(1, sections):
                root_copy(group, step).start()
            root_local(group).start()

    def row_copy(group, step):
        return remote(
            piece(group, tensor),
            piece(group, tensor),
            row_send.at[group, step - 1],
            row_recv.at[group, step - 1],
            section,
            (tensor + 2 * step) % tensors,
        )

    def core_copy(group, step):
        owner = (tensor + tensors - 2 * step) % tensors
        return remote(
            piece(group, owner),
            piece(group, owner),
            core_send.at[group, step],
            core_recv.at[group, step],
            section,
            other_core,
        )

    half = tensors // 2
    for group, root in enumerate(roots):

        @pl.when(section == root)
        def _(group=group):
            root_local(group).wait()

        @pl.when(section != root)
        def _(group=group):
            root_copy(group, 1).wait_recv()

        for step in range(1, half):
            row_copy(group, step).start()
        core_copy(group, 0).start()
    for group in range(groups):
        for step in range(1, half):
            row_copy(group, step).wait_recv()
            core_copy(group, step).start()
    for group in range(groups):
        for step in range(half):
            core_copy(group, step).wait_recv()

    def pair_copy(chunk):
        return remote(
            pair_out.at[chunk],
            pair_in.at[chunk],
            pair_send.at[chunk],
            pair_recv.at[chunk],
            partner,
            tensor,
        )

    def line_copy(chunk, step):
        to_place = (place + step) % line
        return remote(
            line_out.at[chunk, to_place],
            line_in.at[chunk, step - 1],
            line_send.at[chunk, step - 1],
            line_recv.at[chunk, step - 1],
            2 * to_place + parity,
            tensor,
        )

    def visit(turn, carry):
        @pl.when(turn < chunks)
        def _():
            chunk = turn
            weight_copy(chunk).wait()
            product = jnp.dot(captured_v[0], weight_v[chunk, 0], preferred_element_type=F32)
            for group in range(1, groups):
                product += jnp.dot(
                    captured_v[group], weight_v[chunk, group], preferred_element_type=F32
                )
            sums[...] = product.reshape(line, 2, out_rows, width)
            own[chunk] = sums[:, parity]
            pair_out[chunk] = sums[:, 1 - parity].astype(BF16)
            pair_copy(chunk).start()

        @pl.when(turn >= LAG)
        def _():
            chunk = turn - LAG
            pair_copy(chunk).wait_recv()
            summed = own[chunk] + pair_in[chunk].astype(F32)
            own[chunk] = summed
            line_out[chunk] = summed.astype(BF16)
            for step in range(1, line):
                line_copy(chunk, step).start()

        return carry

    lax.fori_loop(0, chunks + LAG, visit, 0)

    def finish(chunk, square_sum):
        for step in range(1, line):
            line_copy(chunk, step).wait_recv()
        summed = own[chunk, place]
        for step in range(1, line):
            summed += line_in[chunk, step - 1].astype(F32)
        final[chunk] = summed
        return square_sum + jnp.sum(summed * summed, axis=1, keepdims=True)

    square_sum = lax.fori_loop(0, chunks, finish, jnp.zeros((out_rows, 1), F32))
    squares[0] = jnp.broadcast_to(square_sum, squares.shape[1:])

    def square_copy(step):
        return remote(
            squares.at[0],
            squares.at[step],
            square_send.at[step - 1],
            square_recv.at[step - 1],
            section,
            (tensor + step) % tensors,
        )

    for step in range(1, tensors):
        square_copy(step).start()
    for step in range(1, tensors):
        square_copy(step).wait_recv()
    square_total = squares[0]
    for step in range(1, tensors):
        square_total += squares[step]
    inverse_rms = lax.rsqrt(square_total[:, 0:1] / (chunks * width * tensors) + 1e-05)
    for chunk in range(chunks):
        columns = slice(chunk * width, (chunk + 1) * width)
        gain = gain_ref[:, columns].astype(F32)
        out_ref[:, columns] = (final[chunk] * inverse_rms * gain).astype(BF16)

    for step in range(1, tensors):
        square_copy(step).wait_send()
    for group, root in enumerate(roots):

        @pl.when(section == root)
        def _(group=group):
            for step in range(1, sections):
                root_copy(group, step).wait_send()

        for step in range(1, half):
            row_copy(group, step).wait_send()
        for step in range(half):
            core_copy(group, step).wait_send()

    def drain(chunk, carry):
        pair_copy(chunk).wait_send()
        for step in range(1, line):
            line_copy(chunk, step).wait_send()
        return carry

    lax.fori_loop(0, chunks, drain, 0)


def merge(captured, weight, gain, sections, tensors):
    rows = captured.shape[0]
    groups, block, columns = weight.shape
    width = min(512, columns)
    chunks = columns // width
    row_total = rows * tensors
    out_rows = row_total // sections
    line = sections // 2
    half = tensors // 2
    dma = pltpu.SemaphoreType.DMA
    anywhere = pl.BlockSpec(memory_space=pl.ANY)
    vmem = pl.BlockSpec(memory_space=pltpu.VMEM)
    return pl.pallas_call(
        functools.partial(merge_kernel, sections, tensors),
        out_shape=jax.ShapeDtypeStruct((out_rows, columns), BF16),
        in_specs=[anywhere, anywhere, vmem],
        out_specs=vmem,
        scratch_shapes=[
            pltpu.VMEM((chunks, groups, block, width), BF16),
            pltpu.VMEM((groups, row_total, block), BF16),
            pltpu.VMEM((line, 2, out_rows, width), F32),
            pltpu.VMEM((chunks, line, out_rows, width), F32),
            pltpu.VMEM((chunks, line, out_rows, width), BF16),
            pltpu.VMEM((chunks, line, out_rows, width), BF16),
            pltpu.VMEM((chunks, line, out_rows, width), BF16),
            pltpu.VMEM((chunks, line - 1, out_rows, width), BF16),
            pltpu.VMEM((chunks, out_rows, width), F32),
            pltpu.VMEM((tensors, out_rows, 128), F32),
            dma((chunks,)),
            dma,
            dma((sections - 1,)),
            dma((groups,)),
            dma((groups, max(half - 1, 1))),
            dma((groups, max(half - 1, 1))),
            dma((groups, half)),
            dma((groups, half)),
            dma((chunks,)),
            dma((chunks,)),
            dma((chunks, line - 1)),
            dma((chunks, line - 1)),
            dma((tensors - 1,)),
            dma((tensors - 1,)),
        ],
        compiler_params=pltpu.CompilerParams(
            collective_id=0, has_side_effects=True, vmem_limit_bytes=61 * 2**20
        ),
        name="merge_layers",
    )(captured, weight, gain)


def solution(mesh):
    sections, tensors = mesh.shape["section"], mesh.shape["tensor"]

    def local(
        tree_queries,
        tree_kv,
        cache_kv,
        residual,
        cache_lengths,
        tree_parents,
        accepted,
        merging_weight,
        merging_gain,
    ):
        verified, captured = attend(
            tree_queries[0],
            tree_kv[0],
            cache_kv[0],
            residual[0],
            cache_lengths,
            tree_parents,
            accepted,
        )
        merged = merge(captured, merging_weight, merging_gain[None, :], sections, tensors)
        tokens = tree_queries.shape[2]
        return verified[None], merged.reshape(-1, tokens, merged.shape[1])

    return jax.shard_map(
        local,
        mesh=mesh,
        in_specs=(
            P("section", "tensor", None, None),
            P("section", "tensor", None, None, None),
            P("section", "tensor", None, None, None),
            P("section", "tensor", None, None),
            P("tensor"),
            P("tensor", None),
            P("tensor"),
            P(None, "section", "tensor"),
            P("tensor"),
        ),
        out_specs=(P("section", "tensor", None, None), P("section", None, "tensor")),
        check_vma=False,
    )
```

```python
import functools

import jax
import jax.numpy as jnp
from jax import lax
from jax.experimental import pallas as pl
from jax.experimental.pallas import tpu as pltpu
from jax.sharding import PartitionSpec as P

KV_HEADS = 8
HEAD_DIM = 128
MESH = pl.DeviceIdType.MESH
F32 = jnp.float32
BF16 = jnp.bfloat16


def attention_kernel(
    lengths_ref,
    parents_ref,
    accepted_ref,
    query_ref,
    cache_ref,
    tree_ref,
    residual_ref,
    verified_ref,
    captured_ref,
    kv_scr,
    head_scr,
    token_scr,
    captured_scr,
):
    row = pl.program_id(0)
    tokens = query_ref.shape[1]
    cached = cache_ref.shape[1]
    own = tree_ref.shape[1]
    span = kv_scr.shape[0]
    heads = query_ref.shape[2] // HEAD_DIM
    group = heads // KV_HEADS
    lines = group * tokens

    kv_scr[0:cached] = cache_ref[0]
    kv_scr[cached:span] = jnp.zeros((span - cached, kv_scr.shape[1]), BF16)
    kv_scr[cached : cached + own] = tree_ref[0]

    for head in range(heads):
        head_scr[head * tokens : (head + 1) * tokens, :] = query_ref[
            0, :, head * HEAD_DIM : (head + 1) * HEAD_DIM
        ].astype(F32)

    bits = [jnp.int32(1)]
    for token in range(1, tokens):
        parent = parents_ref[row, token]
        inherited = jnp.int32(0)
        for earlier in range(token):
            inherited = jnp.where(parent == earlier, bits[earlier], inherited)
        bits.append(inherited | (1 << token))
    token_id = lax.broadcasted_iota(jnp.int32, (lines, span), 0) % tokens
    column = lax.broadcasted_iota(jnp.int32, (lines, span), 1)
    line_bits = jnp.full((lines, span), bits[0], jnp.int32)
    for token in range(1, tokens):
        line_bits = jnp.where(token_id == token, bits[token], line_bits)
    own_index = jnp.clip((column - cached) // 2, 0, 31)
    in_tree = (
        (column >= cached)
        & (column < cached + own)
        & ((lax.shift_right_logical(line_bits, own_index) & 1) == 1)
    )
    in_cache = column < jnp.minimum(2 * lengths_ref[row], cached)
    allowed = (in_cache | in_tree) & (column % 2 == 0)

    factor = HEAD_DIM ** (-0.5)
    scores = []
    for kv in range(KV_HEADS):
        queries = head_scr[kv * lines : (kv + 1) * lines, :].astype(BF16)
        keys = kv_scr[:, kv * HEAD_DIM : (kv + 1) * HEAD_DIM]
        scores.append(
            lax.dot_general(
                queries, keys, (((1,), (1,)), ((), ())), preferred_element_type=F32
            )
        )
    for kv in range(KV_HEADS):
        score = jnp.where(allowed, scores[kv] * factor, -jnp.inf)
        weights = jnp.exp(score - jnp.max(score, axis=1, keepdims=True))
        total = jnp.sum(weights, axis=1, keepdims=True)
        shifted = pltpu.roll(weights, 1, 1).astype(BF16)
        weighted = jnp.dot(
            shifted,
            kv_scr[:, kv * HEAD_DIM : (kv + 1) * HEAD_DIM],
            preferred_element_type=F32,
        )
        head_scr[kv * lines : (kv + 1) * lines, :] = weighted / total

    keep = lax.broadcasted_iota(jnp.int32, (tokens, HEAD_DIM), 0) < accepted_ref[row]
    for head in range(heads):
        features = slice(head * HEAD_DIM, (head + 1) * HEAD_DIM)
        summed = (
            residual_ref[0, :, features].astype(F32)
            + head_scr[head * tokens : (head + 1) * tokens, :]
        )
        verified_ref[0, :, features] = summed.astype(BF16)
        token_scr[:, features] = jnp.where(keep, summed, 0.0)

    shared = captured_scr.shape[1] // tokens
    for place in range(shared):

        @pl.when(row % shared == place)
        def _(place=place):
            captured_scr[row // shared, place * tokens : (place + 1) * tokens, :] = token_scr[...]

    @pl.when(row == pl.num_programs(0) - 1)
    def _():
        captured_ref[...] = captured_scr[...].reshape(captured_ref.shape).astype(BF16)


def attend(queries, tree_kv, cache_kv, residual, lengths, parents, accepted):
    rows, tokens, width = queries.shape
    cached = 2 * cache_kv.shape[1]
    own = 2 * tokens
    span = -(-(cached + own) // 128) * 128
    kv_width = cache_kv.shape[3]
    row_block = lambda *shape: pl.BlockSpec((1,) + shape, lambda r: (r, 0, 0))
    scalars = pl.BlockSpec(memory_space=pltpu.SMEM)
    return pl.pallas_call(
        attention_kernel,
        grid=(rows,),
        out_shape=(
            jax.ShapeDtypeStruct((rows, tokens, width), BF16),
            jax.ShapeDtypeStruct((rows * tokens, width), BF16),
        ),
        in_specs=[
            scalars,
            scalars,
            scalars,
            row_block(tokens, width),
            row_block(cached, kv_width),
            row_block(own, kv_width),
            row_block(tokens, width),
        ],
        out_specs=(
            row_block(tokens, width),
            pl.BlockSpec((rows * tokens, width), lambda r: (0, 0)),
        ),
        scratch_shapes=[
            pltpu.VMEM((span, kv_width), BF16),
            pltpu.VMEM((width // HEAD_DIM * tokens, HEAD_DIM), F32),
            pltpu.VMEM((tokens, width), F32),
            pltpu.VMEM((rows * tokens // 8, 8, width), F32),
        ],
        compiler_params=pltpu.CompilerParams(vmem_limit_bytes=61 * 2**20),
        name="tree_attention",
    )(
        lengths,
        parents,
        accepted,
        queries,
        cache_kv.reshape(rows, cached, kv_width),
        tree_kv.reshape(rows, own, kv_width),
        residual,
    )


LAG = 2
PARTS = 2


def merge_kernel(
    sections,
    tensors,
    captured_ref,
    weight_ref,
    gain_ref,
    out_ref,
    weight_v,
    captured_v,
    sums,
    own,
    pair_out,
    pair_in,
    line_out,
    line_in,
    final,
    squares,
    weight_sem,
    local_sem,
    root_send,
    root_recv,
    row_send,
    row_recv,
    core_send,
    core_recv,
    pair_send,
    pair_recv,
    line_send,
    line_recv,
    square_send,
    square_recv,
):
    section = lax.axis_index("section")
    tensor = lax.axis_index("tensor")
    chunks, groups, block, width = weight_v.shape
    rows = captured_ref.shape[0]
    line = sections // 2
    out_rows, tokens = sums.shape[2], out_ref.shape[1]
    place, parity = section // 2, section % 2
    partner = section + 1 - 2 * parity
    other_core = tensor + 1 - 2 * (tensor % 2)
    part_rows = rows // PARTS
    flip = (2 * place) // line
    order = [turn + flip * (groups - 1 - 2 * turn) for turn in range(groups)]

    def root_of(group):
        return group * (sections // 2) - group // 2

    def remote(src, dst, send, recv, to_section, to_tensor):
        return pltpu.make_async_remote_copy(
            src_ref=src,
            dst_ref=dst,
            send_sem=send,
            recv_sem=recv,
            device_id=(to_section, to_tensor),
            device_id_type=MESH,
        )

    def weight_copy(chunk):
        columns = pl.ds(pl.multiple_of(chunk * width, width), width)
        return pltpu.make_async_copy(
            weight_ref.at[:, :, columns], weight_v.at[chunk], weight_sem.at[chunk]
        )

    barrier = pltpu.get_barrier_semaphore()
    for step in range(1, sections):
        pl.semaphore_signal(
            barrier, inc=1, device_id=((section + step) % sections, tensor), device_id_type=MESH
        )
    for step in range(1, tensors):
        pl.semaphore_signal(
            barrier, inc=1, device_id=(section, (tensor + step) % tensors), device_id_type=MESH
        )
    pl.semaphore_wait(barrier, sections + tensors - 2)

    def piece(group, owner, part):
        first = pl.multiple_of(owner * rows + part * part_rows, part_rows)
        return captured_v.at[group, pl.ds(first, part_rows), :]

    def features(to_section, part):
        return captured_ref.at[
            pl.ds(part * part_rows, part_rows),
            pl.ds(pl.multiple_of(to_section * block, block), block),
        ]

    def root_copy(group, part, step):
        to_section = (section + step) % sections
        return remote(
            features(to_section, part),
            piece(group, tensor, part),
            root_send.at[part, step - 1],
            root_recv.at[group, part],
            to_section,
            tensor,
        )

    def root_local(group, part):
        return pltpu.make_async_copy(
            features(section, part), piece(group, tensor, part), local_sem.at[part]
        )

    for group in range(groups):

        @pl.when(section == root_of(group))
        def _(group=group):
            for part in range(PARTS):
                for step in range(1, sections):
                    root_copy(group, part, step).start()
                root_local(group, part).start()

    for chunk in range(chunks // 2):
        weight_copy(chunk).start()

    def row_copy(group, part, step):
        return remote(
            piece(group, tensor, part),
            piece(group, tensor, part),
            row_send.at[group, part, step - 1],
            row_recv.at[group, part, step - 1],
            section,
            (tensor + 2 * step) % tensors,
        )

    def core_copy(group, part, step):
        owner = (tensor + tensors - 2 * step) % tensors
        return remote(
            piece(group, owner, part),
            piece(group, owner, part),
            core_send.at[group, part, step],
            core_recv.at[group, part, step],
            section,
            other_core,
        )

    half = tensors // 2
    for part in range(PARTS):
        for group in order:

            @pl.when(section == root_of(group))
            def _(group=group, part=part):
                root_local(group, part).wait()

            @pl.when(section != root_of(group))
            def _(group=group, part=part):
                root_copy(group, part, 1).wait_recv()

            for step in range(1, half):
                row_copy(group, part, step).start()
            core_copy(group, part, 0).start()
    for chunk in range(chunks // 2, chunks):
        weight_copy(chunk).start()
    for part in range(PARTS):
        for group in order:
            for step in range(1, half):
                row_copy(group, part, step).wait_recv()
                core_copy(group, part, step).start()
    for part in range(PARTS):
        for group in order:
            for step in range(half):
                core_copy(group, part, step).wait_recv()

    def pair_copy(chunk):
        return remote(
            pair_out.at[chunk],
            pair_in.at[chunk],
            pair_send.at[chunk],
            pair_recv.at[chunk],
            partner,
            tensor,
        )

    def line_copy(chunk, step):
        to_place = (place + step) % line
        return remote(
            line_out.at[chunk, to_place],
            line_in.at[chunk, step - 1],
            line_send.at[chunk, step - 1],
            line_recv.at[chunk, step - 1],
            2 * to_place + parity,
            tensor,
        )

    def visit(turn, carry):
        @pl.when(turn < chunks)
        def _():
            chunk = turn
            weight_copy(chunk).wait()
            product = jnp.dot(captured_v[0], weight_v[chunk, 0], preferred_element_type=F32)
            for group in range(1, groups):
                product += jnp.dot(
                    captured_v[group], weight_v[chunk, group], preferred_element_type=F32
                )
            sums[...] = product.reshape(line, 2, out_rows, width)
            own[chunk] = sums[:, parity]
            pair_out[chunk] = sums[:, 1 - parity].astype(BF16)
            pair_copy(chunk).start()

        @pl.when(turn >= LAG)
        def _():
            chunk = turn - LAG
            pair_copy(chunk).wait_recv()
            summed = own[chunk] + pair_in[chunk].astype(F32)
            own[chunk] = summed
            line_out[chunk] = summed.astype(BF16)
            for step in range(1, line):
                line_copy(chunk, step).start()

        return carry

    lax.fori_loop(0, chunks + LAG, visit, 0)

    def finish(chunk, square_sum):
        for step in range(1, line):
            line_copy(chunk, step).wait_recv()
        summed = own[chunk, place]
        for step in range(1, line):
            summed += line_in[chunk, step - 1].astype(F32)
        final[chunk] = summed
        return square_sum + jnp.sum(summed * summed, axis=1, keepdims=True)

    square_sum = lax.fori_loop(0, chunks, finish, jnp.zeros((out_rows, 1), F32))
    squares[0] = jnp.broadcast_to(square_sum, squares.shape[1:])

    def square_copy(step):
        return remote(
            squares.at[0],
            squares.at[step],
            square_send.at[step - 1],
            square_recv.at[step - 1],
            section,
            (tensor + step) % tensors,
        )

    for step in range(1, tensors):
        square_copy(step).start()
    for step in range(1, tensors):
        square_copy(step).wait_recv()
    square_total = squares[0]
    for step in range(1, tensors):
        square_total += squares[step]
    inverse_rms = lax.rsqrt(square_total[:, 0:1] / (chunks * width * tensors) + 1e-05)
    for chunk in range(chunks):
        columns = slice(chunk * width, (chunk + 1) * width)
        gain = gain_ref[:, columns].astype(F32)
        normed = (final[chunk] * inverse_rms * gain).astype(BF16)
        for row in range(out_rows // tokens):
            out_ref[row, :, columns] = normed[row * tokens : (row + 1) * tokens]

    for step in range(1, tensors):
        square_copy(step).wait_send()
    for group in range(groups):

        @pl.when(section == root_of(group))
        def _(group=group):
            for part in range(PARTS):
                for step in range(1, sections):
                    root_copy(group, part, step).wait_send()

        for part in range(PARTS):
            for step in range(1, half):
                row_copy(group, part, step).wait_send()
            for step in range(half):
                core_copy(group, part, step).wait_send()

    def drain(chunk, carry):
        pair_copy(chunk).wait_send()
        for step in range(1, line):
            line_copy(chunk, step).wait_send()
        return carry

    lax.fori_loop(0, chunks, drain, 0)


def merge(captured, weight, gain, sections, tensors, tokens):
    rows = captured.shape[0]
    groups, block, columns = weight.shape
    width = min(512, columns)
    chunks = columns // width
    row_total = rows * tensors
    out_rows = row_total // sections
    line = sections // 2
    half = tensors // 2
    dma = pltpu.SemaphoreType.DMA
    anywhere = pl.BlockSpec(memory_space=pl.ANY)
    vmem = pl.BlockSpec(memory_space=pltpu.VMEM)
    return pl.pallas_call(
        functools.partial(merge_kernel, sections, tensors),
        out_shape=jax.ShapeDtypeStruct((out_rows // tokens, tokens, columns), BF16),
        in_specs=[anywhere, anywhere, vmem],
        out_specs=vmem,
        scratch_shapes=[
            pltpu.VMEM((chunks, groups, block, width), BF16),
            pltpu.VMEM((groups, row_total, block), BF16),
            pltpu.VMEM((line, 2, out_rows, width), F32),
            pltpu.VMEM((chunks, line, out_rows, width), F32),
            pltpu.VMEM((chunks, line, out_rows, width), BF16),
            pltpu.VMEM((chunks, line, out_rows, width), BF16),
            pltpu.VMEM((chunks, line, out_rows, width), BF16),
            pltpu.VMEM((chunks, line - 1, out_rows, width), BF16),
            pltpu.VMEM((chunks, out_rows, width), F32),
            pltpu.VMEM((tensors, out_rows, 128), F32),
            dma((chunks,)),
            dma((PARTS,)),
            dma((PARTS, sections - 1)),
            dma((groups, PARTS)),
            dma((groups, PARTS, max(half - 1, 1))),
            dma((groups, PARTS, max(half - 1, 1))),
            dma((groups, PARTS, half)),
            dma((groups, PARTS, half)),
            dma((chunks,)),
            dma((chunks,)),
            dma((chunks, line - 1)),
            dma((chunks, line - 1)),
            dma((tensors - 1,)),
            dma((tensors - 1,)),
        ],
        compiler_params=pltpu.CompilerParams(
            collective_id=0, has_side_effects=True, vmem_limit_bytes=61 * 2**20
        ),
        name="merge_layers",
    )(captured, weight, gain)


def solution(mesh):
    sections, tensors = mesh.shape["section"], mesh.shape["tensor"]

    def local(
        tree_queries,
        tree_kv,
        cache_kv,
        residual,
        cache_lengths,
        tree_parents,
        accepted,
        merging_weight,
        merging_gain,
    ):
        verified, captured = attend(
            tree_queries[0],
            tree_kv[0],
            cache_kv[0],
            residual[0],
            cache_lengths,
            tree_parents,
            accepted,
        )
        tokens = tree_queries.shape[2]
        draft_input = merge(
            captured, merging_weight, merging_gain[None, :], sections, tensors, tokens
        )
        return verified[None], draft_input

    return jax.shard_map(
        local,
        mesh=mesh,
        in_specs=(
            P("section", "tensor", None, None),
            P("section", "tensor", None, None, None),
            P("section", "tensor", None, None, None),
            P("section", "tensor", None, None),
            P("tensor"),
            P("tensor", None),
            P("tensor"),
            P(None, "section", "tensor"),
            P("tensor"),
        ),
        out_specs=(P("section", "tensor", None, None), P("section", None, "tensor")),
        check_vma=False,
    )
```

```python
import functools

import jax
import jax.numpy as jnp
from jax import lax
from jax.experimental import pallas as pl
from jax.experimental.pallas import tpu as pltpu
from jax.sharding import PartitionSpec as P

KV_HEADS = 8
HEAD_DIM = 128
MESH = pl.DeviceIdType.MESH
F32 = jnp.float32
BF16 = jnp.bfloat16


def attention_kernel(
    lengths_ref,
    parents_ref,
    accepted_ref,
    query_ref,
    cache_ref,
    tree_ref,
    residual_ref,
    verified_ref,
    captured_ref,
    kv_scr,
    head_scr,
    token_scr,
    captured_scr,
):
    row = pl.program_id(0)
    tokens = query_ref.shape[1]
    cached = cache_ref.shape[1]
    own = tree_ref.shape[1]
    span = kv_scr.shape[0]
    heads = query_ref.shape[2] // HEAD_DIM
    group = heads // KV_HEADS
    lines = group * tokens

    kv_scr[0:cached] = cache_ref[0]
    kv_scr[cached:span] = jnp.zeros((span - cached, kv_scr.shape[1]), BF16)
    kv_scr[cached : cached + own] = tree_ref[0]

    for head in range(heads):
        head_scr[head * tokens : (head + 1) * tokens, :] = query_ref[
            0, :, head * HEAD_DIM : (head + 1) * HEAD_DIM
        ].astype(F32)

    bits = [jnp.int32(1)]
    for token in range(1, tokens):
        parent = parents_ref[row, token]
        inherited = jnp.int32(0)
        for earlier in range(token):
            inherited = jnp.where(parent == earlier, bits[earlier], inherited)
        bits.append(inherited | (1 << token))
    token_id = lax.broadcasted_iota(jnp.int32, (lines, span), 0) % tokens
    column = lax.broadcasted_iota(jnp.int32, (lines, span), 1)
    line_bits = jnp.full((lines, span), bits[0], jnp.int32)
    for token in range(1, tokens):
        line_bits = jnp.where(token_id == token, bits[token], line_bits)
    own_index = jnp.clip((column - cached) // 2, 0, 31)
    in_tree = (
        (column >= cached)
        & (column < cached + own)
        & ((lax.shift_right_logical(line_bits, own_index) & 1) == 1)
    )
    in_cache = column < jnp.minimum(2 * lengths_ref[row], cached)
    allowed = (in_cache | in_tree) & (column % 2 == 0)

    factor = HEAD_DIM ** (-0.5)
    scores = []
    for kv in range(KV_HEADS):
        queries = head_scr[kv * lines : (kv + 1) * lines, :].astype(BF16)
        keys = kv_scr[:, kv * HEAD_DIM : (kv + 1) * HEAD_DIM]
        scores.append(
            lax.dot_general(
                queries, keys, (((1,), (1,)), ((), ())), preferred_element_type=F32
            )
        )
    for kv in range(KV_HEADS):
        score = jnp.where(allowed, scores[kv] * factor, -jnp.inf)
        weights = jnp.exp(score - jnp.max(score, axis=1, keepdims=True))
        total = jnp.sum(weights, axis=1, keepdims=True)
        shifted = pltpu.roll(weights, 1, 1).astype(BF16)
        weighted = jnp.dot(
            shifted,
            kv_scr[:, kv * HEAD_DIM : (kv + 1) * HEAD_DIM],
            preferred_element_type=F32,
        )
        head_scr[kv * lines : (kv + 1) * lines, :] = weighted / total

    keep = lax.broadcasted_iota(jnp.int32, (tokens, HEAD_DIM), 0) < accepted_ref[row]
    for head in range(heads):
        features = slice(head * HEAD_DIM, (head + 1) * HEAD_DIM)
        summed = (
            residual_ref[0, :, features].astype(F32)
            + head_scr[head * tokens : (head + 1) * tokens, :]
        )
        verified_ref[0, :, features] = summed.astype(BF16)
        token_scr[:, features] = jnp.where(keep, summed, 0.0)

    shared = captured_scr.shape[1] // tokens
    for place in range(shared):

        @pl.when(row % shared == place)
        def _(place=place):
            captured_scr[row // shared, place * tokens : (place + 1) * tokens, :] = token_scr[...]

    @pl.when(row == pl.num_programs(0) - 1)
    def _():
        captured_ref[...] = captured_scr[...].reshape(captured_ref.shape).astype(BF16)


def attend(queries, tree_kv, cache_kv, residual, lengths, parents, accepted):
    rows, tokens, width = queries.shape
    cached = 2 * cache_kv.shape[1]
    own = 2 * tokens
    span = -(-(cached + own) // 128) * 128
    kv_width = cache_kv.shape[3]
    row_block = lambda *shape: pl.BlockSpec((1,) + shape, lambda r: (r, 0, 0))
    scalars = pl.BlockSpec(memory_space=pltpu.SMEM)
    return pl.pallas_call(
        attention_kernel,
        grid=(rows,),
        out_shape=(
            jax.ShapeDtypeStruct((rows, tokens, width), BF16),
            jax.ShapeDtypeStruct((rows * tokens, width), BF16),
        ),
        in_specs=[
            scalars,
            scalars,
            scalars,
            row_block(tokens, width),
            row_block(cached, kv_width),
            row_block(own, kv_width),
            row_block(tokens, width),
        ],
        out_specs=(
            row_block(tokens, width),
            pl.BlockSpec((rows * tokens, width), lambda r: (0, 0)),
        ),
        scratch_shapes=[
            pltpu.VMEM((span, kv_width), BF16),
            pltpu.VMEM((width // HEAD_DIM * tokens, HEAD_DIM), F32),
            pltpu.VMEM((tokens, width), F32),
            pltpu.VMEM((rows * tokens // 8, 8, width), F32),
        ],
        compiler_params=pltpu.CompilerParams(vmem_limit_bytes=61 * 2**20),
        name="tree_attention",
    )(
        lengths,
        parents,
        accepted,
        queries,
        cache_kv.reshape(rows, cached, kv_width),
        tree_kv.reshape(rows, own, kv_width),
        residual,
    )


LAG = 2
PARTS = 2


def merge_kernel(
    sections,
    tensors,
    captured_ref,
    weight_ref,
    gain_ref,
    out_ref,
    weight_v,
    captured_v,
    sums,
    own,
    pair_out,
    pair_in,
    line_out,
    line_in,
    final,
    squares,
    partial,
    weight_sem,
    local_sem,
    root_send,
    root_recv,
    row_send,
    row_recv,
    core_send,
    core_recv,
    pair_send,
    pair_recv,
    line_send,
    line_recv,
    square_send,
    square_recv,
):
    section = lax.axis_index("section")
    tensor = lax.axis_index("tensor")
    chunks, groups, block, width = weight_v.shape
    rows = captured_ref.shape[0]
    line = sections // 2
    out_rows, tokens = sums.shape[2], out_ref.shape[1]
    place, parity = section // 2, section % 2
    partner = section + 1 - 2 * parity
    other_core = tensor + 1 - 2 * (tensor % 2)
    part_rows = rows // PARTS
    flip = (2 * place) // line
    order = [turn + flip * (groups - 1 - 2 * turn) for turn in range(groups)]

    def root_of(group):
        return group * (sections // 2) - group // 2

    def remote(src, dst, send, recv, to_section, to_tensor):
        return pltpu.make_async_remote_copy(
            src_ref=src,
            dst_ref=dst,
            send_sem=send,
            recv_sem=recv,
            device_id=(to_section, to_tensor),
            device_id_type=MESH,
        )

    def weight_copy(chunk):
        columns = pl.ds(pl.multiple_of(chunk * width, width), width)
        return pltpu.make_async_copy(
            weight_ref.at[:, :, columns], weight_v.at[chunk], weight_sem.at[chunk]
        )

    barrier = pltpu.get_barrier_semaphore()
    for step in range(1, sections):
        pl.semaphore_signal(
            barrier, inc=1, device_id=((section + step) % sections, tensor), device_id_type=MESH
        )
    for step in range(1, tensors):
        pl.semaphore_signal(
            barrier, inc=1, device_id=(section, (tensor + step) % tensors), device_id_type=MESH
        )
    pl.semaphore_wait(barrier, sections + tensors - 2)

    def piece(group, owner, part):
        first = pl.multiple_of(owner * rows + part * part_rows, part_rows)
        return captured_v.at[group, pl.ds(first, part_rows), :]

    def features(to_section, part):
        return captured_ref.at[
            pl.ds(part * part_rows, part_rows),
            pl.ds(pl.multiple_of(to_section * block, block), block),
        ]

    def root_copy(group, part, step):
        to_section = (section + step) % sections
        return remote(
            features(to_section, part),
            piece(group, tensor, part),
            root_send.at[part, step - 1],
            root_recv.at[group, part],
            to_section,
            tensor,
        )

    def root_local(group, part):
        return pltpu.make_async_copy(
            features(section, part), piece(group, tensor, part), local_sem.at[part]
        )

    for group in range(groups):

        @pl.when(section == root_of(group))
        def _(group=group):
            for part in range(PARTS):
                for step in range(1, sections):
                    root_copy(group, part, step).start()
                root_local(group, part).start()

    for chunk in range(chunks // 2):
        weight_copy(chunk).start()

    def row_copy(group, part, step):
        return remote(
            piece(group, tensor, part),
            piece(group, tensor, part),
            row_send.at[group, part, step - 1],
            row_recv.at[group, part, step - 1],
            section,
            (tensor + 2 * step) % tensors,
        )

    def core_copy(group, part, step):
        owner = (tensor + tensors - 2 * step) % tensors
        return remote(
            piece(group, owner, part),
            piece(group, owner, part),
            core_send.at[group, part, step],
            core_recv.at[group, part, step],
            section,
            other_core,
        )

    half = tensors // 2
    for part in range(PARTS):
        for group in order:

            @pl.when(section == root_of(group))
            def _(group=group, part=part):
                root_local(group, part).wait()

            @pl.when(section != root_of(group))
            def _(group=group, part=part):
                root_copy(group, part, 1).wait_recv()

            for step in range(1, half):
                row_copy(group, part, step).start()
            core_copy(group, part, 0).start()
    for chunk in range(chunks // 2, chunks):
        weight_copy(chunk).start()
    for turn, group in enumerate(order):
        for part in range(PARTS):
            for step in range(1, half):
                row_copy(group, part, step).wait_recv()
                core_copy(group, part, step).start()
        for part in range(PARTS):
            for step in range(half):
                core_copy(group, part, step).wait_recv()
        if turn < groups - 1:

            def accumulate(chunk, carry, turn=turn, group=group):
                if turn == 0:
                    weight_copy(chunk).wait()
                product = jnp.dot(
                    captured_v[group], weight_v[chunk, group], preferred_element_type=F32
                )
                partial[chunk] = product if turn == 0 else partial[chunk] + product
                return carry

            lax.fori_loop(0, chunks, accumulate, 0)

    def pair_copy(chunk):
        return remote(
            pair_out.at[chunk],
            pair_in.at[chunk],
            pair_send.at[chunk],
            pair_recv.at[chunk],
            partner,
            tensor,
        )

    def line_copy(chunk, step):
        to_place = (place + step) % line
        return remote(
            line_out.at[chunk, to_place],
            line_in.at[chunk, step - 1],
            line_send.at[chunk, step - 1],
            line_recv.at[chunk, step - 1],
            2 * to_place + parity,
            tensor,
        )

    def visit(turn, carry):
        @pl.when(turn < chunks)
        def _():
            chunk = turn
            group = order[-1]
            product = partial[chunk] + jnp.dot(
                captured_v[group], weight_v[chunk, group], preferred_element_type=F32
            )
            sums[...] = product.reshape(line, 2, out_rows, width)
            own[chunk] = sums[:, parity]
            pair_out[chunk] = sums[:, 1 - parity].astype(BF16)
            pair_copy(chunk).start()

        @pl.when(turn >= LAG)
        def _():
            chunk = turn - LAG
            pair_copy(chunk).wait_recv()
            summed = own[chunk] + pair_in[chunk].astype(F32)
            own[chunk] = summed
            line_out[chunk] = summed.astype(BF16)
            for step in range(1, line):
                line_copy(chunk, step).start()

        return carry

    lax.fori_loop(0, chunks + LAG, visit, 0)

    def finish(chunk, square_sum):
        for step in range(1, line):
            line_copy(chunk, step).wait_recv()
        summed = own[chunk, place]
        for step in range(1, line):
            summed += line_in[chunk, step - 1].astype(F32)
        final[chunk] = summed
        return square_sum + jnp.sum(summed * summed, axis=1, keepdims=True)

    square_sum = lax.fori_loop(0, chunks, finish, jnp.zeros((out_rows, 1), F32))
    squares[0] = jnp.broadcast_to(square_sum, squares.shape[1:])

    def square_copy(step):
        return remote(
            squares.at[0],
            squares.at[step],
            square_send.at[step - 1],
            square_recv.at[step - 1],
            section,
            (tensor + step) % tensors,
        )

    for step in range(1, tensors):
        square_copy(step).start()
    for step in range(1, tensors):
        square_copy(step).wait_recv()
    square_total = squares[0]
    for step in range(1, tensors):
        square_total += squares[step]
    inverse_rms = lax.rsqrt(square_total[:, 0:1] / (chunks * width * tensors) + 1e-05)
    for chunk in range(chunks):
        columns = slice(chunk * width, (chunk + 1) * width)
        gain = gain_ref[:, columns].astype(F32)
        normed = (final[chunk] * inverse_rms * gain).astype(BF16)
        for row in range(out_rows // tokens):
            out_ref[row, :, columns] = normed[row * tokens : (row + 1) * tokens]

    for step in range(1, tensors):
        square_copy(step).wait_send()
    for group in range(groups):

        @pl.when(section == root_of(group))
        def _(group=group):
            for part in range(PARTS):
                for step in range(1, sections):
                    root_copy(group, part, step).wait_send()

        for part in range(PARTS):
            for step in range(1, half):
                row_copy(group, part, step).wait_send()
            for step in range(half):
                core_copy(group, part, step).wait_send()

    def drain(chunk, carry):
        pair_copy(chunk).wait_send()
        for step in range(1, line):
            line_copy(chunk, step).wait_send()
        return carry

    lax.fori_loop(0, chunks, drain, 0)


def merge(captured, weight, gain, sections, tensors, tokens):
    rows = captured.shape[0]
    groups, block, columns = weight.shape
    width = min(512, columns)
    chunks = columns // width
    row_total = rows * tensors
    out_rows = row_total // sections
    line = sections // 2
    half = tensors // 2
    dma = pltpu.SemaphoreType.DMA
    anywhere = pl.BlockSpec(memory_space=pl.ANY)
    vmem = pl.BlockSpec(memory_space=pltpu.VMEM)
    return pl.pallas_call(
        functools.partial(merge_kernel, sections, tensors),
        out_shape=jax.ShapeDtypeStruct((out_rows // tokens, tokens, columns), BF16),
        in_specs=[anywhere, anywhere, vmem],
        out_specs=vmem,
        scratch_shapes=[
            pltpu.VMEM((chunks, groups, block, width), BF16),
            pltpu.VMEM((groups, row_total, block), BF16),
            pltpu.VMEM((line, 2, out_rows, width), F32),
            pltpu.VMEM((chunks, line, out_rows, width), F32),
            pltpu.VMEM((chunks, line, out_rows, width), BF16),
            pltpu.VMEM((chunks, line, out_rows, width), BF16),
            pltpu.VMEM((chunks, line, out_rows, width), BF16),
            pltpu.VMEM((chunks, line - 1, out_rows, width), BF16),
            pltpu.VMEM((chunks, out_rows, width), F32),
            pltpu.VMEM((tensors, out_rows, 128), F32),
            pltpu.VMEM((chunks, row_total, width), F32),
            dma((chunks,)),
            dma((PARTS,)),
            dma((PARTS, sections - 1)),
            dma((groups, PARTS)),
            dma((groups, PARTS, max(half - 1, 1))),
            dma((groups, PARTS, max(half - 1, 1))),
            dma((groups, PARTS, half)),
            dma((groups, PARTS, half)),
            dma((chunks,)),
            dma((chunks,)),
            dma((chunks, line - 1)),
            dma((chunks, line - 1)),
            dma((tensors - 1,)),
            dma((tensors - 1,)),
        ],
        compiler_params=pltpu.CompilerParams(
            collective_id=0, has_side_effects=True, vmem_limit_bytes=61 * 2**20
        ),
        name="merge_layers",
    )(captured, weight, gain)


def solution(mesh):
    sections, tensors = mesh.shape["section"], mesh.shape["tensor"]

    def local(
        tree_queries,
        tree_kv,
        cache_kv,
        residual,
        cache_lengths,
        tree_parents,
        accepted,
        merging_weight,
        merging_gain,
    ):
        verified, captured = attend(
            tree_queries[0],
            tree_kv[0],
            cache_kv[0],
            residual[0],
            cache_lengths,
            tree_parents,
            accepted,
        )
        tokens = tree_queries.shape[2]
        draft_input = merge(
            captured, merging_weight, merging_gain[None, :], sections, tensors, tokens
        )
        return verified[None], draft_input

    return jax.shard_map(
        local,
        mesh=mesh,
        in_specs=(
            P("section", "tensor", None, None),
            P("section", "tensor", None, None, None),
            P("section", "tensor", None, None, None),
            P("section", "tensor", None, None),
            P("tensor"),
            P("tensor", None),
            P("tensor"),
            P(None, "section", "tensor"),
            P("tensor"),
        ),
        out_specs=(P("section", "tensor", None, None), P("section", None, "tensor")),
        check_vma=False,
    )
```
